32 devices in a mesh: groups: 2 (over y), ep: 8 (over z, x), sub: 2 (over core).
Axes of the slice: x: 2, y: 2, z: 4, core: 2. Of those that a mesh axis runs over, the one named last changes fastest.
Arguments:
- queries: bfloat16 [128, 4, 128, 576], P(('groups', 'ep', 'sub')), parts along dimension 0, may hold values from -8.25 to 8.25, as said below
- draft_keys: bfloat16 [128, 4, 576], P(('groups', 'ep', 'sub')), parts along dimension 0, may hold values from -6 to 6, as said below
- page_pool: bfloat16 [8192, 16, 576], P(('groups', 'ep', 'sub')), parts along dimension 0, may hold values from -6 to 6
- send_slot: int32 [32, 16], P(('groups', 'ep', 'sub')), parts along dimension 0, may hold values from -1 to 255, as said below
- page_table: int32 [128, 64], P(('groups', 'ep', 'sub')), parts along dimension 0, may hold values from 0 to 271, as said below
- cache_length: int32 [128], P(('groups', 'ep', 'sub')), parts along dimension 0, may hold values from 1 to 1024, as said below
- value_up_matrix: bfloat16 [128, 512, 128], P(('ep', 'sub')), may hold values from -0.25 to 0.25
Outputs:
- head_values: bfloat16 [128, 4, 16384], P(('groups', 'ep', 'sub')), parts along dimension 0
The draws below stay inside these ranges and needn't reach their ends.
There are 2 independent parts, one for each index of `groups`. The reference program is written for one: setup_inputs(seed, part) draws one part's arguments, and reference() takes and returns one part's arrays. A program takes and returns all parts, laid end to end along the dimension named above; an argument that names none is the same for every part. Nothing has to cross between parts.
Inputs may be any that keep to these rules, and one draw needn't show every extreme that they name: `queries`: queries of order one. `draft_keys`: keys of order one. `send_slot`: each device sends exactly 15 pages, at most one to any other device and none to itself, each page at most once, and each device receives exactly 15 pages; a page that a device sends is not named in its own page_table rows. `page_table`: an entry e < 256 names page e of the device's own pages, an entry 256 + p the page received from device p; the 4 rows of one device name every page that the device holds after the migration (its unsent pages and the 15 received ones) exactly once. `cache_length`: some request holds 1024 accepted tokens and some holds 1.
All inputs are finite; a program needn't handle non-finite values.
Results may differ from the reference program's by a relative error of at most 0.0057.
Values may be sent and summed in bfloat16 or wider, within the bound.
A program may use at most 128 MiB of HBM per device.

```python
import jax
import jax.numpy as jnp
from jax import lax

HEAD_TOTAL = 128
LATENT_WIDTH = 512
VALUE_WIDTH = 128
KW = 576
DRAFT = 4
PAGE = 16
REQ_DEV = 4
CTX = 1024
PEERS = 16
REQS = 64
PAGES_REQ = 64
POOL = 256
MIG = 15


def migration_plan(key):
    candidates = jnp.arange(1, PEERS, dtype=jnp.int32)
    ranking = jax.random.permutation(jax.random.fold_in(key, 11), PEERS - 1).astype(jnp.int32)
    ranking = jnp.where(candidates == 1, -2, jnp.where(candidates == PEERS // 2, -1, ranking))
    ordered = candidates[jnp.argsort(ranking, stable=True)]
    offsets = ordered[:MIG].astype(jnp.int32)

    def one_device(device):
        ordering = jax.random.permutation(jax.random.fold_in(jax.random.fold_in(key, 12), device), POOL).astype(jnp.int32)
        shuffle = jax.random.permutation(jax.random.fold_in(jax.random.fold_in(key, 13), device), POOL)
        targets = (device + offsets) % PEERS
        sending = jnp.full((PEERS,), -1, jnp.int32).at[targets].set(ordering[:MIG])
        sources = (device - offsets) % PEERS
        holding = jnp.concatenate([ordering[MIG:], POOL + sources]).astype(jnp.int32)
        return (sending, holding[shuffle].reshape(REQ_DEV, PAGES_REQ))
    return jax.vmap(one_device)(jnp.arange(PEERS, dtype=jnp.int32))


def draw_send_slot(key, part):
    sending, tables = migration_plan(key)
    return sending


def draw_page_table(key, part):
    sending, tables = migration_plan(key)
    return tables.reshape(REQS, PAGES_REQ)


def draw_cache_length(key, part):
    key = jax.random.fold_in(key, 31)
    lengths = jax.random.randint(jax.random.fold_in(key, 1), (REQS,), 1, CTX + 1)
    longest = jax.random.randint(jax.random.fold_in(key, 2), (), 0, REQS)
    second = (longest + 1 + jax.random.randint(jax.random.fold_in(key, 3), (), 0, REQS - 1)) % REQS
    return lengths.at[longest].set(CTX).at[second].set(1).astype(jnp.int32)


def draw_queries(key, part):
    key_own = jax.random.fold_in(key, 51)
    values_drawn = jnp.clip(jax.random.normal(key_own, (REQS, DRAFT, HEAD_TOTAL, KW), jnp.float32), -6.0, 6.0)
    return values_drawn.astype(jnp.bfloat16)


def draw_draft_keys(key, part):
    key_own = jax.random.fold_in(key, 52)
    values_drawn = jnp.clip(jax.random.normal(key_own, (REQS, DRAFT, KW), jnp.float32), -6.0, 6.0)
    return values_drawn.astype(jnp.bfloat16)


def levels(key, extent, split, low, high):
    level, own = 1.0, jax.random.fold_in(key, 6)
    for axis_at, shards_of in split:
        heights = jnp.exp(jax.random.uniform(jax.random.fold_in(own, axis_at), (shards_of,), jnp.float32, low / len(split), high / len(split)))
        level = level * jnp.repeat(heights, extent[axis_at] // shards_of).reshape([-1 if axis == axis_at else 1 for axis in range(len(extent))])
    return level


def scatter_about(stream_key, extent, spread, reach, split=(), kind=jnp.bfloat16):
    result = spread * jax.random.normal(stream_key, extent, jnp.float32)
    if split:
        result = result * levels(stream_key, extent, split, -0.22, 0.18)
    return jnp.clip(result, -reach, reach).astype(kind)


def setup_inputs(seed: int = 0, part: int = 0) -> dict:
    splits = jax.random.split(jax.random.key(seed), 8)
    own_keys = jax.random.split(jax.random.fold_in(splits[7], part), 8)
    queries = draw_queries(jax.random.fold_in(jax.random.fold_in(splits[7], part), 71), part)
    draft_keys = draw_draft_keys(jax.random.fold_in(jax.random.fold_in(splits[7], part), 71), part)
    page_pool = scatter_about(own_keys[2], (PEERS * POOL, PAGE, KW), 1.0, 6.0, ((0, 16),))
    send_slot = draw_send_slot(jax.random.fold_in(jax.random.fold_in(splits[7], part), 71), part)
    page_table = draw_page_table(jax.random.fold_in(jax.random.fold_in(splits[7], part), 71), part)
    cache_length = draw_cache_length(jax.random.fold_in(jax.random.fold_in(splits[7], part), 71), part)
    value_up_matrix = scatter_about(splits[6], (HEAD_TOTAL, LATENT_WIDTH, VALUE_WIDTH), LATENT_WIDTH ** -0.5, 0.25, ((0, 16),))
    return dict(queries=queries, draft_keys=draft_keys, page_pool=page_pool, send_slot=send_slot, page_table=page_table, cache_length=cache_length, value_up_matrix=value_up_matrix)


score_scale = 192 ** -0.5


def attend(request_query, draft_key, page_rows, length, page_store):
    draft_token_count, head_number, key_width = request_query.shape
    cache_keys = page_store[page_rows].reshape(-1, key_width)
    context = cache_keys.shape[0]
    key_rows_all = jnp.concatenate([cache_keys, draft_key], axis=0)
    score_rows = request_query.reshape(draft_token_count * head_number, key_width)
    scores = jnp.dot(score_rows, key_rows_all.T, preferred_element_type=jnp.float32) * score_scale
    column_index = jnp.arange(context + draft_token_count, dtype=jnp.int32)[None, :]
    row_draft = (jnp.arange(draft_token_count * head_number, dtype=jnp.int32) // head_number)[:, None]
    live_mask = jnp.where(column_index < context, column_index < length, column_index - context <= row_draft)
    scores = jnp.where(live_mask, scores, -jnp.inf)
    row_top = jnp.max(scores, axis=1, keepdims=True)
    exponent = jnp.exp(scores - row_top)
    row_total = jnp.sum(exponent, axis=1, keepdims=True)
    softmax_weight = (exponent / row_total).astype(jnp.bfloat16)
    latent_state = jnp.dot(softmax_weight, key_rows_all[:, :LATENT_WIDTH], preferred_element_type=jnp.float32).astype(jnp.bfloat16)
    return latent_state.reshape(draft_token_count, head_number, LATENT_WIDTH)


def reference(queries, draft_keys, page_pool, send_slot, page_table, cache_length, value_up_matrix):
    device_pages = page_pool.reshape(PEERS, POOL, PAGE, KW)
    device_queries = queries.reshape(PEERS, REQ_DEV, DRAFT, HEAD_TOTAL, KW)
    device_drafts = draft_keys.reshape(PEERS, REQ_DEV, DRAFT, KW)
    device_tables = page_table.reshape(PEERS, REQ_DEV, PAGES_REQ)
    device_lengths = cache_length.reshape(PEERS, REQ_DEV)
    peer_index = jnp.arange(PEERS, dtype=jnp.int32)
    up_weights = value_up_matrix.astype(jnp.float32)

    def one_device(device):
        sent_pages = send_slot[:, device]
        received = device_pages[peer_index, jnp.maximum(sent_pages, 0)]
        received = jnp.where((sent_pages >= 0)[:, None, None], received, jnp.zeros((), page_pool.dtype))
        page_store = jnp.concatenate([device_pages[device], received], axis=0)

        def one_request(inputs):
            latent_state = attend(inputs[0], inputs[1], inputs[2], inputs[3], page_store)
            mixed_heads = jnp.einsum("jhc,hcv->jhv", latent_state.astype(jnp.float32), up_weights)
            return mixed_heads.astype(jnp.bfloat16).reshape(DRAFT, HEAD_TOTAL * VALUE_WIDTH)

        return lax.map(one_request, (device_queries[device], device_drafts[device], device_tables[device], device_lengths[device]))

    values = lax.map(one_device, jnp.arange(PEERS, dtype=jnp.int32))
    return values.reshape(REQS, DRAFT, HEAD_TOTAL * VALUE_WIDTH)
```

```python
import functools
import math

import jax
import jax.numpy as jnp
from jax import lax
from jax.experimental import pallas as pl
from jax.experimental.pallas import tpu as pltpu
from jax.sharding import PartitionSpec as P

LATENT_WIDTH = 512
AXES = ("ep", "sub")
EXP2_SCALE = 192 ** (-0.5) * math.log2(math.e)
DEAD = -1e30


def attend_kernel(length_ref, table_ref, query_ref, draft_ref, pool_ref, received_ref, latent_ref, keys, bias):
    request = pl.program_id(0)
    requests, rows, width = keys.shape
    page, _, pool_pages = pool_ref.shape
    peers = received_ref.shape[1]
    draft = draft_ref.shape[1]
    heads = query_ref.shape[3]
    pages = table_ref.shape[0] // requests
    context = pages * page

    @pl.when(request == 0)
    def _():
        table = table_ref[...]
        column = lax.broadcasted_iota(jnp.int32, (requests * pages, pool_pages), 1)
        pick_own = jnp.where(column == table, 1.0, 0.0).astype(jnp.bfloat16)
        column = lax.broadcasted_iota(jnp.int32, (requests * pages, peers), 1)
        pick_received = jnp.where(column + pool_pages == table, 1.0, 0.0).astype(jnp.bfloat16)
        for place in range(page):
            got = lax.dot_general(
                pick_own, pool_ref[place], (((1,), (1,)), ((), ())), preferred_element_type=jnp.float32
            ) + jnp.dot(pick_received, received_ref[place], preferred_element_type=jnp.float32)
            keys[:, place * pages : (place + 1) * pages, :] = got.astype(jnp.bfloat16).reshape(
                requests, pages, width
            )
        for r in range(requests):
            keys[r, context:rows, :] = jnp.concatenate(
                [draft_ref[r].astype(jnp.float32), jnp.zeros((rows - context - draft, width), jnp.float32)], axis=0
            ).astype(jnp.bfloat16)

    row = lax.broadcasted_iota(jnp.int32, (context, heads), 0)
    position = lax.rem(row, pages) * page + lax.div(row, pages)
    bias[...] = jnp.where(position < length_ref[request], 0.0, DEAD)
    late = lax.broadcasted_iota(jnp.int32, (rows - context, heads), 0)
    for pair in range(0, draft, 2):
        query = jnp.concatenate([query_ref[0, pair], query_ref[0, pair + 1]], axis=1)
        scores = jnp.dot(keys[request], query, preferred_element_type=jnp.float32)
        weights = []
        for j in range(2):
            part = scores[:, j * heads : (j + 1) * heads]
            early = part[:context] + bias[...]
            own = jnp.where(late <= pair + j, part[context:], DEAD)
            top = jnp.maximum(
                jnp.max(early, axis=0, keepdims=True), jnp.max(own, axis=0, keepdims=True)
            )
            early = jnp.exp2((early - top) * EXP2_SCALE)
            own = jnp.exp2((own - top) * EXP2_SCALE)
            total = jnp.sum(early, axis=0, keepdims=True) + jnp.sum(own, axis=0, keepdims=True)
            inverse = 1.0 / total
            weights.append(
                jnp.concatenate(
                    [(early * inverse).astype(jnp.bfloat16), (own * inverse).astype(jnp.bfloat16)], axis=0
                )
            )
        latent = lax.dot_general(
            jnp.concatenate(weights, axis=1),
            keys[request, :, :LATENT_WIDTH],
            (((0,), (0,)), ((), ())),
            preferred_element_type=jnp.float32,
        ).astype(jnp.bfloat16)
        latent_ref[0, pair] = latent[:heads]
        latent_ref[0, pair + 1] = latent[heads:]


def per_device(
    queries, draft_keys, page_pool, send_slot, page_table, cache_length, value_up_matrix
):
    requests, draft, heads, width = queries.shape
    pool_pages, page, _ = page_pool.shape
    peers = send_slot.shape[1]
    pages = page_table.shape[1]
    choose = (send_slot[0][:, None] == jnp.arange(pool_pages, dtype=jnp.int32)[None, :]).astype(jnp.bfloat16)
    outgoing = jnp.einsum("qp,psk->qsk", choose, page_pool, preferred_element_type=jnp.bfloat16)
    received = lax.all_to_all(outgoing, AXES, split_axis=0, concat_axis=0, tiled=True)
    received = received.transpose(1, 0, 2)
    rows = pages * page + 16
    vmem = pl.BlockSpec(memory_space=pltpu.VMEM)
    latent = pl.pallas_call(
        attend_kernel,
        grid=(requests,),
        out_shape=jax.ShapeDtypeStruct((requests, draft, heads, LATENT_WIDTH), jnp.bfloat16),
        in_specs=[
            pl.BlockSpec(memory_space=pltpu.SMEM),
            vmem,
            pl.BlockSpec((1, draft, width, heads), lambda r: (r, 0, 0, 0)),
            vmem,
            vmem,
            vmem,
        ],
        out_specs=pl.BlockSpec((1, draft, heads, LATENT_WIDTH), lambda r: (r, 0, 0, 0)),
        scratch_shapes=[
            pltpu.VMEM((requests, rows, width), jnp.bfloat16),
            pltpu.VMEM((pages * page, heads), jnp.float32),
        ],
        compiler_params=pltpu.CompilerParams(vmem_limit_bytes=48 * 2**20),
        name="attend",
    )(
        cache_length,
        page_table.reshape(-1, 1),
        queries.swapaxes(2, 3),
        draft_keys,
        page_pool.transpose(1, 2, 0),
        received,
    )
    shares = lax.all_to_all(
        latent.reshape(requests * draft, heads, LATENT_WIDTH), AXES, split_axis=1, concat_axis=0, tiled=True
    )
    mixed = jnp.einsum(
        "rhc,hcv->rhv", shares, value_up_matrix, preferred_element_type=jnp.float32
    ).astype(jnp.bfloat16)
    mixed = lax.all_to_all(mixed, AXES, split_axis=0, concat_axis=1, tiled=True)
    return mixed.reshape(requests, draft, -1)


def solution(mesh):
    placed = (
        P(("groups", "ep", "sub"), None, None, None),
        P(("groups", "ep", "sub"), None, None),
        P(("groups", "ep", "sub"), None, None),
        P(("groups", "ep", "sub"), None),
        P(("groups", "ep", "sub"), None),
        P(("groups", "ep", "sub")),
        P(("ep", "sub"), None, None),
    )
    return jax.shard_map(
        per_device,
        mesh=mesh,
        in_specs=placed,
        out_specs=P(("groups", "ep", "sub"), None, None),
        check_vma=False,
    )
```

```python
import functools
import math

import jax
import jax.numpy as jnp
from jax import lax
from jax.experimental import pallas as pl
from jax.experimental.pallas import tpu as pltpu
from jax.sharding import PartitionSpec as P

LATENT_WIDTH = 512
AXES = ("ep", "sub")
EXP2_SCALE = 192 ** (-0.5) * math.log2(math.e)
DEAD = -1e30


def exchange_kernel(
    groups_of,
    length_ref,
    table_ref,
    query_ref,
    draft_ref,
    pool_ref,
    outgoing_ref,
    matrix_ref,
    back_ref,
    keys,
    bias,
    arrived_pages,
    matrix,
    sending,
    arrived,
    mixed,
    page_sent,
    page_got,
    latent_sent,
    latent_got,
    mixed_sent,
    mixed_got,
):
    requests, rows, width = keys.shape
    page, _, pool_pages = pool_ref.shape
    peers = outgoing_ref.shape[0]
    draft = draft_ref.shape[1]
    heads = query_ref.shape[3]
    pages = table_ref.shape[0] // requests
    context = pages * page
    own_heads, latent_width, value_width = matrix_ref.shape
    outer, inner = groups_of
    me = lax.axis_index("ep") * inner + lax.axis_index("sub")

    def place_of(peer):
        return {"ep": lax.div(peer, inner), "sub": lax.rem(peer, inner)}

    def copy_to(source, target, sent, got, peer):
        return pltpu.make_async_remote_copy(
            src_ref=source,
            dst_ref=target,
            send_sem=sent,
            recv_sem=got,
            device_id=place_of(peer),
            device_id_type=pl.DeviceIdType.MESH,
        )

    barrier = pltpu.get_barrier_semaphore()

    @pl.loop(1, peers)
    def _(step):
        pl.semaphore_signal(
            barrier,
            inc=1,
            device_id=place_of(lax.rem(me + step, peers)),
            device_id_type=pl.DeviceIdType.MESH,
        )

    pl.semaphore_wait(barrier, peers - 1)

    @pl.loop(1, peers)
    def _(step):
        peer = lax.rem(me + step, peers)
        copy_to(outgoing_ref.at[peer], arrived_pages.at[me], page_sent, page_got, peer).start()

    arrived_pages[me] = outgoing_ref[me]
    for h in range(own_heads):
        matrix[:, h * value_width : (h + 1) * value_width] = matrix_ref[h]

    table = table_ref[...]
    column = lax.broadcasted_iota(jnp.int32, (requests * pages, pool_pages), 1)
    pick_own = jnp.where(column == table, 1.0, 0.0).astype(jnp.bfloat16)

    @pl.loop(0, page)
    def _(place):
        got = lax.dot_general(
            pick_own, pool_ref[place], (((1,), (1,)), ((), ())), preferred_element_type=jnp.float32
        ).astype(jnp.bfloat16)
        start = pl.multiple_of(place * pages, pages)
        keys[:, pl.ds(start, pages), :] = got.reshape(requests, pages, width)

    for r in range(requests):
        keys[r, context:rows, :] = jnp.concatenate(
            [draft_ref[r].astype(jnp.float32), jnp.zeros((rows - context - draft, width), jnp.float32)], axis=0
        ).astype(jnp.bfloat16)

    all_pages = pl.ds(0, peers - 1)
    copy_to(outgoing_ref.at[all_pages], arrived_pages.at[all_pages], page_sent, page_got, me).wait_recv()
    column = lax.broadcasted_iota(jnp.int32, (requests * pages, peers * page), 1)
    page_match = lax.div(column, page) + pool_pages == table
    column_place = lax.rem(column, page)
    received = arrived_pages[...].reshape(peers * page, width)

    @pl.loop(0, page)
    def _(place):
        pick = jnp.where(page_match & (column_place == place), 1.0, 0.0).astype(jnp.bfloat16)
        got = jnp.dot(pick, received, preferred_element_type=jnp.float32).astype(jnp.bfloat16)
        start = pl.multiple_of(place * pages, pages)
        keys[:, pl.ds(start, pages), :] += got.reshape(requests, pages, width)

    @pl.loop(0, requests)
    def _(request):
        row = lax.broadcasted_iota(jnp.int32, (context, heads), 0)
        position = lax.rem(row, pages) * page + lax.div(row, pages)
        bias[...] = jnp.where(position < length_ref[request], 0.0, DEAD)
        late = lax.broadcasted_iota(jnp.int32, (rows - context, heads), 0)
        for pair in range(0, draft, 2):
            query = jnp.concatenate([query_ref[request, pair], query_ref[request, pair + 1]], axis=1)
            scores = jnp.dot(keys[request], query, preferred_element_type=jnp.float32)
            weights = []
            for j in range(2):
                part = scores[:, j * heads : (j + 1) * heads]
                early = part[:context] + bias[...]
                own = jnp.where(late <= pair + j, part[context:], DEAD)
                top = jnp.maximum(
                    jnp.max(early, axis=0, keepdims=True), jnp.max(own, axis=0, keepdims=True)
                )
                early = jnp.exp2((early - top) * EXP2_SCALE)
                own = jnp.exp2((own - top) * EXP2_SCALE)
                total = jnp.sum(early, axis=0, keepdims=True) + jnp.sum(own, axis=0, keepdims=True)
                inverse = 1.0 / total
                weights.append(
                    jnp.concatenate(
                        [(early * inverse).astype(jnp.bfloat16), (own * inverse).astype(jnp.bfloat16)], axis=0
                    )
                )
            latent = lax.dot_general(
                jnp.concatenate(weights, axis=1),
                keys[request, :, :latent_width],
                (((0,), (0,)), ((), ())),
                preferred_element_type=jnp.float32,
            )
            for p in range(peers):
                first = p * own_heads
                both = jnp.concatenate(
                    [latent[first : first + own_heads], latent[heads + first : heads + first + own_heads]], axis=0
                )
                sending[request, p, pair * own_heads : (pair + 2) * own_heads, :] = both.astype(jnp.bfloat16)

        @pl.loop(1, peers)
        def _(step):
            peer = lax.rem(me + step, peers)
            copy_to(
                sending.at[request, peer],
                arrived.at[request, me],
                latent_sent.at[request],
                latent_got.at[request],
                peer,
            ).start()

        arrived[request, me] = sending[request, me]

    @pl.loop(0, requests)
    def _(request):
        copy_to(
            sending.at[request, all_pages],
            arrived.at[request, all_pages],
            latent_sent.at[request],
            latent_got.at[request],
            me,
        ).wait_recv()
        block = draft * own_heads
        every = jnp.dot(
            arrived[request].reshape(peers * block, latent_width), matrix[...], preferred_element_type=jnp.float32
        )
        head = lax.rem(lax.broadcasted_iota(jnp.int32, (peers * block, value_width), 0), own_heads)
        chosen = every[:, :value_width]
        for h in range(1, own_heads):
            chosen = jnp.where(head == h, every[:, h * value_width : (h + 1) * value_width], chosen)
        mixed[request] = chosen.astype(jnp.bfloat16).reshape(peers, block, value_width)

        @pl.loop(1, peers)
        def _(step):
            peer = lax.rem(me + step, peers)
            copy_to(
                mixed.at[request, peer],
                back_ref.at[request, me],
                mixed_sent.at[request],
                mixed_got.at[request],
                peer,
            ).start()

        back_ref[request, me] = mixed[request, me]

    copy_to(outgoing_ref.at[all_pages], arrived_pages.at[all_pages], page_sent, page_got, me).wait_send()

    @pl.loop(0, requests)
    def _(request):
        copy_to(
            sending.at[request, all_pages],
            arrived.at[request, all_pages],
            latent_sent.at[request],
            latent_got.at[request],
            me,
        ).wait_send()
        copy_to(
            mixed.at[request, all_pages],
            back_ref.at[request, all_pages],
            mixed_sent.at[request],
            mixed_got.at[request],
            me,
        ).wait()


def per_device(
    groups_of, queries, draft_keys, page_pool, send_slot, page_table, cache_length, value_up_matrix
):
    requests, draft, heads, width = queries.shape
    pool_pages, page, _ = page_pool.shape
    peers = send_slot.shape[1]
    pages = page_table.shape[1]
    own_heads, _, value_width = value_up_matrix.shape
    choose = (send_slot[0][:, None] == jnp.arange(pool_pages, dtype=jnp.int32)[None, :]).astype(jnp.bfloat16)
    outgoing = jnp.einsum("qp,psk->qsk", choose, page_pool, preferred_element_type=jnp.bfloat16)
    rows = pages * page + 16
    block = draft * own_heads
    vmem = pl.BlockSpec(memory_space=pltpu.VMEM)
    back = pl.pallas_call(
        functools.partial(exchange_kernel, groups_of),
        out_shape=jax.ShapeDtypeStruct((requests, peers, block, value_width), jnp.bfloat16),
        in_specs=[pl.BlockSpec(memory_space=pltpu.SMEM)] + [vmem] * 6,
        out_specs=vmem,
        scratch_shapes=[
            pltpu.VMEM((requests, rows, width), jnp.bfloat16),
            pltpu.VMEM((pages * page, heads), jnp.float32),
            pltpu.VMEM((peers, page, width), jnp.bfloat16),
            pltpu.VMEM((LATENT_WIDTH, own_heads * value_width), jnp.bfloat16),
            pltpu.VMEM((requests, peers, block, LATENT_WIDTH), jnp.bfloat16),
            pltpu.VMEM((requests, peers, block, LATENT_WIDTH), jnp.bfloat16),
            pltpu.VMEM((requests, peers, block, value_width), jnp.bfloat16),
            pltpu.SemaphoreType.DMA,
            pltpu.SemaphoreType.DMA,
            pltpu.SemaphoreType.DMA((requests,)),
            pltpu.SemaphoreType.DMA((requests,)),
            pltpu.SemaphoreType.DMA((requests,)),
            pltpu.SemaphoreType.DMA((requests,)),
        ],
        compiler_params=pltpu.CompilerParams(
            collective_id=0, has_side_effects=True, vmem_limit_bytes=48 * 2**20
        ),
        name="exchange",
    )(
        cache_length,
        page_table.reshape(-1, 1),
        queries.swapaxes(2, 3),
        draft_keys,
        page_pool.transpose(1, 2, 0),
        outgoing,
        value_up_matrix,
    )
    back = back.reshape(requests, peers, draft, own_heads * value_width)
    return back.swapaxes(1, 2).reshape(requests, draft, heads * value_width)


def solution(mesh):
    placed = (
        P(("groups", "ep", "sub"), None, None, None),
        P(("groups", "ep", "sub"), None, None),
        P(("groups", "ep", "sub"), None, None),
        P(("groups", "ep", "sub"), None),
        P(("groups", "ep", "sub"), None),
        P(("groups", "ep", "sub")),
        P(("ep", "sub"), None, None),
    )
    return jax.shard_map(
        functools.partial(per_device, (mesh.shape["ep"], mesh.shape["sub"])),
        mesh=mesh,
        in_specs=placed,
        out_specs=P(("groups", "ep", "sub"), None, None),
        check_vma=False,
    )
```

```python
import functools
import math

import jax
import jax.numpy as jnp
from jax import lax
from jax.experimental import pallas as pl
from jax.experimental.pallas import tpu as pltpu
from jax.sharding import PartitionSpec as P

LATENT_WIDTH = 512
AXES = ("ep", "sub")
EXP2_SCALE = 192 ** (-0.5) * math.log2(math.e)
DEAD = -1e30


def exchange_kernel(
    groups_of,
    length_ref,
    table_ref,
    query_ref,
    draft_ref,
    pool_ref,
    outgoing_ref,
    matrix_ref,
    back_ref,
    keys,
    bias,
    arrived_pages,
    matrix,
    sending,
    arrived,
    mixed,
    page_sent,
    page_got,
    latent_sent,
    latent_got,
    mixed_sent,
    mixed_got,
    far_matrix,
    weights_sent,
    weights_got,
    swap_sent,
    swap_got,
):
    requests, rows, width = keys.shape
    page, _, pool_pages = pool_ref.shape
    peers = outgoing_ref.shape[0]
    draft = draft_ref.shape[1]
    heads = query_ref.shape[3]
    pages = table_ref.shape[0] // requests
    context = pages * page
    own_heads, latent_width, value_width = matrix_ref.shape
    groups, outer, inner = groups_of
    me = lax.axis_index("ep") * inner + lax.axis_index("sub")
    near = peers // 2
    side = lax.div(me, near)
    seat = lax.rem(me, near)
    group = lax.axis_index("groups")
    share = latent_width // groups

    def place_of(peer):
        return {"ep": lax.div(peer, inner), "sub": lax.rem(peer, inner)}

    def copy_to(source, target, sent, got, peer):
        return pltpu.make_async_remote_copy(
            src_ref=source,
            dst_ref=target,
            send_sem=sent,
            recv_sem=got,
            device_id=place_of(peer),
            device_id_type=pl.DeviceIdType.MESH,
        )

    barrier = pltpu.get_barrier_semaphore()

    @pl.loop(1, peers)
    def _(step):
        pl.semaphore_signal(
            barrier,
            inc=1,
            device_id=place_of(lax.rem(me + step, peers)),
            device_id_type=pl.DeviceIdType.MESH,
        )

    for step in range(1, groups):
        pl.semaphore_signal(
            barrier,
            inc=1,
            device_id={"groups": lax.rem(group + step, groups)},
            device_id_type=pl.DeviceIdType.MESH,
        )
    pl.semaphore_wait(barrier, peers + groups - 2)

    @pl.loop(1, peers)
    def _(step):
        peer = lax.rem(me + step, peers)
        copy_to(outgoing_ref.at[peer], arrived_pages.at[me], page_sent, page_got, peer).start()

    own_share = pl.ds(pl.multiple_of(group * share, share), share)
    across = pltpu.make_async_remote_copy(
        src_ref=matrix_ref.at[:, own_share],
        dst_ref=far_matrix.at[:, own_share],
        send_sem=weights_sent,
        recv_sem=weights_got,
        device_id={"ep": lax.rem(lax.axis_index("ep") + outer // 2, outer)},
        device_id_type=pl.DeviceIdType.MESH,
    )
    across.start()
    swaps = [
        pltpu.make_async_remote_copy(
            src_ref=far_matrix.at[:, own_share],
            dst_ref=far_matrix.at[:, own_share],
            send_sem=swap_sent.at[step],
            recv_sem=swap_got.at[step],
            device_id={"groups": lax.rem(group + step, groups)},
            device_id_type=pl.DeviceIdType.MESH,
        )
        for step in range(1, groups)
    ]

    arrived_pages[me] = outgoing_ref[me]
    for h in range(own_heads):
        matrix[side, :, h * value_width : (h + 1) * value_width] = matrix_ref[h]

    table = table_ref[...]
    column = lax.broadcasted_iota(jnp.int32, (requests * pages, pool_pages), 1)
    pick_own = jnp.where(column == table, 1.0, 0.0).astype(jnp.bfloat16)

    @pl.loop(0, page)
    def _(place):
        got = lax.dot_general(
            pick_own, pool_ref[place], (((1,), (1,)), ((), ())), preferred_element_type=jnp.float32
        ).astype(jnp.bfloat16)
        start = pl.multiple_of(place * pages, pages)
        keys[:, pl.ds(start, pages), :] = got.reshape(requests, pages, width)

    for r in range(requests):
        keys[r, context:rows, :] = jnp.concatenate(
            [draft_ref[r].astype(jnp.float32), jnp.zeros((rows - context - draft, width), jnp.float32)], axis=0
        ).astype(jnp.bfloat16)

    all_pages = pl.ds(0, peers - 1)
    copy_to(outgoing_ref.at[all_pages], arrived_pages.at[all_pages], page_sent, page_got, me).wait_recv()
    column = lax.broadcasted_iota(jnp.int32, (requests * pages, peers * page), 1)
    page_match = lax.div(column, page) + pool_pages == table
    column_place = lax.rem(column, page)
    received = arrived_pages[...].reshape(peers * page, width)

    @pl.loop(0, page)
    def _(place):
        pick = jnp.where(page_match & (column_place == place), 1.0, 0.0).astype(jnp.bfloat16)
        got = jnp.dot(pick, received, preferred_element_type=jnp.float32).astype(jnp.bfloat16)
        start = pl.multiple_of(place * pages, pages)
        keys[:, pl.ds(start, pages), :] += got.reshape(requests, pages, width)

    @pl.loop(0, requests)
    def _(request):
        row = lax.broadcasted_iota(jnp.int32, (context, heads), 0)
        position = lax.rem(row, pages) * page + lax.div(row, pages)
        bias[...] = jnp.where(position < length_ref[request], 0.0, DEAD)
        late = lax.broadcasted_iota(jnp.int32, (rows - context, heads), 0)
        for pair in range(0, draft, 2):
            query = jnp.concatenate([query_ref[request, pair], query_ref[request, pair + 1]], axis=1)
            scores = jnp.dot(keys[request], query, preferred_element_type=jnp.float32)
            weights = []
            for j in range(2):
                part = scores[:, j * heads : (j + 1) * heads]
                early = part[:context] + bias[...]
                own = jnp.where(late <= pair + j, part[context:], DEAD)
                top = jnp.maximum(
                    jnp.max(early, axis=0, keepdims=True), jnp.max(own, axis=0, keepdims=True)
                )
                early = jnp.exp2((early - top) * EXP2_SCALE)
                own = jnp.exp2((own - top) * EXP2_SCALE)
                total = jnp.sum(early, axis=0, keepdims=True) + jnp.sum(own, axis=0, keepdims=True)
                inverse = 1.0 / total
                weights.append(
                    jnp.concatenate(
                        [(early * inverse).astype(jnp.bfloat16), (own * inverse).astype(jnp.bfloat16)], axis=0
                    )
                )
            latent = lax.dot_general(
                jnp.concatenate(weights, axis=1),
                keys[request, :, :latent_width],
                (((0,), (0,)), ((), ())),
                preferred_element_type=jnp.float32,
            )
            for p in range(peers):
                first = p * own_heads
                both = jnp.concatenate(
                    [latent[first : first + own_heads], latent[heads + first : heads + first + own_heads]], axis=0
                )
                sending[request, p, pair * own_heads : (pair + 2) * own_heads, :] = both.astype(jnp.bfloat16)

        @pl.loop(1, near)
        def _(step):
            other = lax.rem(seat + step, near)
            for half in range(2):
                copy_to(
                    sending.at[request, half * near + other],
                    arrived.at[request, half * near + seat],
                    latent_sent.at[request],
                    latent_got.at[request],
                    side * near + other,
                ).start()

        for half in range(2):
            arrived[request, half * near + seat] = sending[request, half * near + seat]

        @pl.when(request == max(requests - 2, 0))
        def _():
            across.wait_recv()
            for swap in swaps:
                swap.start()

    for swap in swaps:
        swap.wait_recv()
    for h in range(own_heads):
        matrix[1 - side, :, h * value_width : (h + 1) * value_width] = far_matrix[h]
    near_pages = pl.ds(0, 2 * near - 2)

    @pl.loop(0, requests)
    def _(request):
        copy_to(
            sending.at[request, near_pages],
            arrived.at[request, near_pages],
            latent_sent.at[request],
            latent_got.at[request],
            me,
        ).wait_recv()
        block = draft * own_heads
        head = lax.rem(lax.broadcasted_iota(jnp.int32, (near * block, value_width), 0), own_heads)
        for half in range(2):
            every = jnp.dot(
                arrived[request, half * near : (half + 1) * near].reshape(near * block, latent_width),
                matrix[half],
                preferred_element_type=jnp.float32,
            )
            chosen = every[:, :value_width]
            for h in range(1, own_heads):
                chosen = jnp.where(head == h, every[:, h * value_width : (h + 1) * value_width], chosen)
            mixed[request, half * near : (half + 1) * near] = chosen.astype(jnp.bfloat16).reshape(
                near, block, value_width
            )

        @pl.loop(1, near)
        def _(step):
            other = lax.rem(seat + step, near)
            for half in range(2):
                copy_to(
                    mixed.at[request, half * near + other],
                    back_ref.at[request, half * near + seat],
                    mixed_sent.at[request],
                    mixed_got.at[request],
                    side * near + other,
                ).start()

        for half in range(2):
            back_ref[request, half * near + seat] = mixed[request, half * near + seat]

    across.wait_send()
    for swap in swaps:
        swap.wait_send()
    copy_to(outgoing_ref.at[all_pages], arrived_pages.at[all_pages], page_sent, page_got, me).wait_send()

    @pl.loop(0, requests)
    def _(request):
        copy_to(
            sending.at[request, near_pages],
            arrived.at[request, near_pages],
            latent_sent.at[request],
            latent_got.at[request],
            me,
        ).wait_send()
        copy_to(
            mixed.at[request, near_pages],
            back_ref.at[request, near_pages],
            mixed_sent.at[request],
            mixed_got.at[request],
            me,
        ).wait()


def per_device(
    groups_of, queries, draft_keys, page_pool, send_slot, page_table, cache_length, value_up_matrix
):
    requests, draft, heads, width = queries.shape
    pool_pages, page, _ = page_pool.shape
    peers = send_slot.shape[1]
    pages = page_table.shape[1]
    own_heads, _, value_width = value_up_matrix.shape
    choose = (send_slot[0][:, None] == jnp.arange(pool_pages, dtype=jnp.int32)[None, :]).astype(jnp.bfloat16)
    outgoing = jnp.einsum("qp,psk->qsk", choose, page_pool, preferred_element_type=jnp.bfloat16)
    rows = pages * page + 16
    block = draft * own_heads
    vmem = pl.BlockSpec(memory_space=pltpu.VMEM)
    back = pl.pallas_call(
        functools.partial(exchange_kernel, groups_of),
        out_shape=jax.ShapeDtypeStruct((requests, peers, block, value_width), jnp.bfloat16),
        in_specs=[pl.BlockSpec(memory_space=pltpu.SMEM)] + [vmem] * 6,
        out_specs=vmem,
        scratch_shapes=[
            pltpu.VMEM((requests, rows, width), jnp.bfloat16),
            pltpu.VMEM((pages * page, heads), jnp.float32),
            pltpu.VMEM((peers, page, width), jnp.bfloat16),
            pltpu.VMEM((2, LATENT_WIDTH, own_heads * value_width), jnp.bfloat16),
            pltpu.VMEM((requests, peers, block, LATENT_WIDTH), jnp.bfloat16),
            pltpu.VMEM((requests, peers, block, LATENT_WIDTH), jnp.bfloat16),
            pltpu.VMEM((requests, peers, block, value_width), jnp.bfloat16),
            pltpu.SemaphoreType.DMA,
            pltpu.SemaphoreType.DMA,
            pltpu.SemaphoreType.DMA((requests,)),
            pltpu.SemaphoreType.DMA((requests,)),
            pltpu.SemaphoreType.DMA((requests,)),
            pltpu.SemaphoreType.DMA((requests,)),
            pltpu.VMEM(value_up_matrix.shape, jnp.bfloat16),
            pltpu.SemaphoreType.DMA,
            pltpu.SemaphoreType.DMA,
            pltpu.SemaphoreType.DMA((groups_of[0],)),
            pltpu.SemaphoreType.DMA((groups_of[0],)),
        ],
        compiler_params=pltpu.CompilerParams(
            collective_id=0, has_side_effects=True, vmem_limit_bytes=48 * 2**20
        ),
        name="exchange",
    )(
        cache_length,
        page_table.reshape(-1, 1),
        queries.swapaxes(2, 3),
        draft_keys,
        page_pool.transpose(1, 2, 0),
        outgoing,
        value_up_matrix,
    )
    back = back.reshape(requests, peers, draft, own_heads * value_width)
    return back.swapaxes(1, 2).reshape(requests, draft, heads * value_width)


def solution(mesh):
    placed = (
        P(("groups", "ep", "sub"), None, None, None),
        P(("groups", "ep", "sub"), None, None),
        P(("groups", "ep", "sub"), None, None),
        P(("groups", "ep", "sub"), None),
        P(("groups", "ep", "sub"), None),
        P(("groups", "ep", "sub")),
        P(("ep", "sub"), None, None),
    )
    return jax.shard_map(
        functools.partial(per_device, (mesh.shape["groups"], mesh.shape["ep"], mesh.shape["sub"])),
        mesh=mesh,
        in_specs=placed,
        out_specs=P(("groups", "ep", "sub"), None, None),
        check_vma=False,
    )
```

```python
import functools
import math

import jax
import jax.numpy as jnp
from jax import lax
from jax.experimental import pallas as pl
from jax.experimental.pallas import tpu as pltpu
from jax.sharding import PartitionSpec as P

LATENT_WIDTH = 512
AXES = ("ep", "sub")
EXP2_SCALE = 192 ** (-0.5) * math.log2(math.e)
DEAD = -1e30


def exchange_kernel(
    groups_of,
    length_ref,
    table_ref,
    query_ref,
    draft_ref,
    pool_ref,
    outgoing_ref,
    matrix_ref,
    back_ref,
    keys,
    bias,
    arrived_pages,
    matrix,
    sending,
    arrived,
    mixed,
    page_sent,
    page_got,
    latent_sent,
    latent_got,
    mixed_sent,
    mixed_got,
    far_matrix,
    weights_sent,
    weights_got,
    swap_sent,
    swap_got,
):
    requests, rows, width = keys.shape
    page, _, pool_pages = pool_ref.shape
    peers = outgoing_ref.shape[0]
    draft = draft_ref.shape[1]
    heads = query_ref.shape[3]
    pages = table_ref.shape[0] // requests
    context = pages * page
    own_heads, latent_width, value_width = matrix_ref.shape
    groups, outer, inner = groups_of
    me = lax.axis_index("ep") * inner + lax.axis_index("sub")
    near = peers // 2
    side = lax.div(me, near)
    seat = lax.rem(me, near)
    group = lax.axis_index("groups")
    share = latent_width // groups

    def place_of(peer):
        return {"ep": lax.div(peer, inner), "sub": lax.rem(peer, inner)}

    def copy_to(source, target, sent, got, peer):
        return pltpu.make_async_remote_copy(
            src_ref=source,
            dst_ref=target,
            send_sem=sent,
            recv_sem=got,
            device_id=place_of(peer),
            device_id_type=pl.DeviceIdType.MESH,
        )

    barrier = pltpu.get_barrier_semaphore()

    @pl.loop(1, peers)
    def _(step):
        pl.semaphore_signal(
            barrier,
            inc=1,
            device_id=place_of(lax.rem(me + step, peers)),
            device_id_type=pl.DeviceIdType.MESH,
        )

    for step in range(1, groups):
        pl.semaphore_signal(
            barrier,
            inc=1,
            device_id={"groups": lax.rem(group + step, groups)},
            device_id_type=pl.DeviceIdType.MESH,
        )
    pl.semaphore_wait(barrier, peers + groups - 2)

    @pl.loop(1, peers)
    def _(step):
        peer = lax.rem(me + step, peers)
        copy_to(outgoing_ref.at[peer], arrived_pages.at[me], page_sent, page_got, peer).start()

    own_share = pl.ds(pl.multiple_of(group * share, share), share)
    across = pltpu.make_async_remote_copy(
        src_ref=matrix_ref.at[:, own_share],
        dst_ref=far_matrix.at[:, own_share],
        send_sem=weights_sent,
        recv_sem=weights_got,
        device_id={"ep": lax.rem(lax.axis_index("ep") + outer // 2, outer)},
        device_id_type=pl.DeviceIdType.MESH,
    )
    across.start()
    swaps = [
        pltpu.make_async_remote_copy(
            src_ref=far_matrix.at[:, own_share],
            dst_ref=far_matrix.at[:, own_share],
            send_sem=swap_sent.at[step],
            recv_sem=swap_got.at[step],
            device_id={"groups": lax.rem(group + step, groups)},
            device_id_type=pl.DeviceIdType.MESH,
        )
        for step in range(1, groups)
    ]

    arrived_pages[me] = outgoing_ref[me]
    for h in range(own_heads):
        matrix[side, :, h * value_width : (h + 1) * value_width] = matrix_ref[h]

    table = table_ref[...]
    column = lax.broadcasted_iota(jnp.int32, (requests * pages, pool_pages), 1)
    pick_own = jnp.where(column == table, 1.0, 0.0).astype(jnp.bfloat16)

    @pl.loop(0, page)
    def _(place):
        got = lax.dot_general(
            pick_own, pool_ref[place], (((1,), (1,)), ((), ())), preferred_element_type=jnp.float32
        ).astype(jnp.bfloat16)
        start = pl.multiple_of(place * pages, pages)
        keys[:, pl.ds(start, pages), :] = got.reshape(requests, pages, width)

    for r in range(requests):
        keys[r, context:rows, :] = jnp.concatenate(
            [draft_ref[r].astype(jnp.float32), jnp.zeros((rows - context - draft, width), jnp.float32)], axis=0
        ).astype(jnp.bfloat16)

    all_pages = pl.ds(0, peers - 1)
    copy_to(outgoing_ref.at[all_pages], arrived_pages.at[all_pages], page_sent, page_got, me).wait_recv()
    column = lax.broadcasted_iota(jnp.int32, (requests * pages, peers * page), 1)
    page_match = lax.div(column, page) + pool_pages == table
    column_place = lax.rem(column, page)
    received = arrived_pages[...].reshape(peers * page, width)

    @pl.loop(0, page)
    def _(place):
        pick = jnp.where(page_match & (column_place == place), 1.0, 0.0).astype(jnp.bfloat16)
        got = jnp.dot(pick, received, preferred_element_type=jnp.float32).astype(jnp.bfloat16)
        start = pl.multiple_of(place * pages, pages)
        keys[:, pl.ds(start, pages), :] += got.reshape(requests, pages, width)

    @pl.loop(0, requests)
    def _(request):
        row = lax.broadcasted_iota(jnp.int32, (context, heads), 0)
        position = lax.rem(row, pages) * page + lax.div(row, pages)
        bias[...] = jnp.where(position < length_ref[request], 0.0, DEAD)
        late = lax.broadcasted_iota(jnp.int32, (rows - context, heads), 0)
        for pair in range(0, draft, 2):
            query = jnp.concatenate([query_ref[request, pair], query_ref[request, pair + 1]], axis=1)
            scores = jnp.dot(keys[request], query, preferred_element_type=jnp.float32)
            weights = []
            for j in range(2):
                part = scores[:, j * heads : (j + 1) * heads]
                early = part[:context] + bias[...]
                own = jnp.where(late <= pair + j, part[context:], DEAD)
                top = jnp.maximum(
                    jnp.max(early, axis=0, keepdims=True), jnp.max(own, axis=0, keepdims=True)
                )
                early = jnp.exp2((early - top) * EXP2_SCALE)
                own = jnp.exp2((own - top) * EXP2_SCALE)
                total = jnp.sum(early, axis=0, keepdims=True) + jnp.sum(own, axis=0, keepdims=True)
                inverse = 1.0 / total
                weights.append(
                    jnp.concatenate(
                        [(early * inverse).astype(jnp.bfloat16), (own * inverse).astype(jnp.bfloat16)], axis=0
                    )
                )
            latent = lax.dot_general(
                jnp.concatenate(weights, axis=1),
                keys[request, :, :latent_width],
                (((0,), (0,)), ((), ())),
                preferred_element_type=jnp.float32,
            )
            for p in range(peers):
                first = p * own_heads
                both = jnp.concatenate(
                    [latent[first : first + own_heads], latent[heads + first : heads + first + own_heads]], axis=0
                )
                sending[request, p, pair * own_heads : (pair + 2) * own_heads, :] = both.astype(jnp.bfloat16)

        @pl.loop(1, near)
        def _(step):
            other = lax.rem(seat + step, near)
            for half in range(2):
                copy_to(
                    sending.at[request, half * near + other],
                    arrived.at[request, half * near + seat],
                    latent_sent.at[request],
                    latent_got.at[request],
                    side * near + other,
                ).start()

        for half in range(2):
            arrived[request, half * near + seat] = sending[request, half * near + seat]

    near_pages = pl.ds(0, 2 * near - 2)
    block = draft * own_heads

    def raise_values(request, half):
        seats = pl.ds(half * near, near)
        every = jnp.dot(
            arrived[request, seats].reshape(near * block, latent_width),
            matrix[half],
            preferred_element_type=jnp.float32,
        )
        head = lax.rem(lax.broadcasted_iota(jnp.int32, (near * block, value_width), 0), own_heads)
        chosen = every[:, :value_width]
        for h in range(1, own_heads):
            chosen = jnp.where(head == h, every[:, h * value_width : (h + 1) * value_width], chosen)
        mixed[request, seats] = chosen.astype(jnp.bfloat16).reshape(near, block, value_width)

        @pl.loop(1, near)
        def _(step):
            other = lax.rem(seat + step, near)
            copy_to(
                mixed.at[request, half * near + other],
                back_ref.at[request, half * near + seat],
                mixed_sent.at[request],
                mixed_got.at[request],
                side * near + other,
            ).start()

        back_ref[request, half * near + seat] = mixed[request, half * near + seat]

    @pl.loop(0, requests)
    def _(request):
        copy_to(
            sending.at[request, near_pages],
            arrived.at[request, near_pages],
            latent_sent.at[request],
            latent_got.at[request],
            me,
        ).wait_recv()
        raise_values(request, side)

        @pl.when(request == 0)
        def _():
            across.wait_recv()
            for swap in swaps:
                swap.start()

    for swap in swaps:
        swap.wait_recv()
    for h in range(own_heads):
        matrix[1 - side, :, h * value_width : (h + 1) * value_width] = far_matrix[h]

    @pl.loop(0, requests)
    def _(request):
        raise_values(request, 1 - side)

    across.wait_send()
    for swap in swaps:
        swap.wait_send()
    copy_to(outgoing_ref.at[all_pages], arrived_pages.at[all_pages], page_sent, page_got, me).wait_send()

    @pl.loop(0, requests)
    def _(request):
        copy_to(
            sending.at[request, near_pages],
            arrived.at[request, near_pages],
            latent_sent.at[request],
            latent_got.at[request],
            me,
        ).wait_send()
        copy_to(
            mixed.at[request, near_pages],
            back_ref.at[request, near_pages],
            mixed_sent.at[request],
            mixed_got.at[request],
            me,
        ).wait()


def per_device(
    groups_of, queries, draft_keys, page_pool, send_slot, page_table, cache_length, value_up_matrix
):
    requests, draft, heads, width = queries.shape
    pool_pages, page, _ = page_pool.shape
    peers = send_slot.shape[1]
    pages = page_table.shape[1]
    own_heads, _, value_width = value_up_matrix.shape
    choose = (send_slot[0][:, None] == jnp.arange(pool_pages, dtype=jnp.int32)[None, :]).astype(jnp.bfloat16)
    outgoing = jnp.einsum("qp,psk->qsk", choose, page_pool, preferred_element_type=jnp.bfloat16)
    rows = pages * page + 16
    block = draft * own_heads
    vmem = pl.BlockSpec(memory_space=pltpu.VMEM)
    back = pl.pallas_call(
        functools.partial(exchange_kernel, groups_of),
        out_shape=jax.ShapeDtypeStruct((requests, peers, block, value_width), jnp.bfloat16),
        in_specs=[pl.BlockSpec(memory_space=pltpu.SMEM)] + [vmem] * 6,
        out_specs=vmem,
        scratch_shapes=[
            pltpu.VMEM((requests, rows, width), jnp.bfloat16),
            pltpu.VMEM((pages * page, heads), jnp.float32),
            pltpu.VMEM((peers, page, width), jnp.bfloat16),
            pltpu.VMEM((2, LATENT_WIDTH, own_heads * value_width), jnp.bfloat16),
            pltpu.VMEM((requests, peers, block, LATENT_WIDTH), jnp.bfloat16),
            pltpu.VMEM((requests, peers, block, LATENT_WIDTH), jnp.bfloat16),
            pltpu.VMEM((requests, peers, block, value_width), jnp.bfloat16),
            pltpu.SemaphoreType.DMA,
            pltpu.SemaphoreType.DMA,
            pltpu.SemaphoreType.DMA((requests,)),
            pltpu.SemaphoreType.DMA((requests,)),
            pltpu.SemaphoreType.DMA((requests,)),
            pltpu.SemaphoreType.DMA((requests,)),
            pltpu.VMEM(value_up_matrix.shape, jnp.bfloat16),
            pltpu.SemaphoreType.DMA,
            pltpu.SemaphoreType.DMA,
            pltpu.SemaphoreType.DMA((groups_of[0],)),
            pltpu.SemaphoreType.DMA((groups_of[0],)),
        ],
        compiler_params=pltpu.CompilerParams(
            collective_id=0, has_side_effects=True, vmem_limit_bytes=48 * 2**20
        ),
        name="exchange",
    )(
        cache_length,
        page_table.reshape(-1, 1),
        queries.swapaxes(2, 3),
        draft_keys,
        page_pool.transpose(1, 2, 0),
        outgoing,
        value_up_matrix,
    )
    back = back.reshape(requests, peers, draft, own_heads * value_width)
    return back.swapaxes(1, 2).reshape(requests, draft, heads * value_width)


def solution(mesh):
    placed = (
        P(("groups", "ep", "sub"), None, None, None),
        P(("groups", "ep", "sub"), None, None),
        P(("groups", "ep", "sub"), None, None),
        P(("groups", "ep", "sub"), None),
        P(("groups", "ep", "sub"), None),
        P(("groups", "ep", "sub")),
        P(("ep", "sub"), None, None),
    )
    return jax.shard_map(
        functools.partial(per_device, (mesh.shape["groups"], mesh.shape["ep"], mesh.shape["sub"])),
        mesh=mesh,
        in_specs=placed,
        out_specs=P(("groups", "ep", "sub"), None, None),
        check_vma=False,
    )
```
